32 devices in a mesh: groups: 2 (over x), row: 16 (over z, y, core).
Axes of the slice: x: 2, y: 2, z: 4, core: 2. Of those that a mesh axis runs over, the one named last changes fastest.
Arguments:
- object_field: float32 [2, 8192, 512], P(None, ('groups', 'row')), parts along dimension 1, may hold values from -5 to 5
- probe_wave: float32 [2, 512, 256], P(None, 'groups'), parts along dimension 1, may hold values from -5 to 5
- patterns: float32 [256, 256, 256], P(('groups', 'row')), parts along dimension 0, may hold values from 0.1 to 4
- positions: int32 [256, 2], P(('groups', 'row')), parts along dimension 0, may hold values from -128 to 3967, as said below
- counts: int32 [32], P('groups'), parts along dimension 0, may hold values from 1 to 8, as said below
Outputs:
- object_grad: float32 [2, 8192, 512], P(None, ('groups', 'row')), parts along dimension 1
- probe_grad: float32 [2, 512, 256], P(None, 'groups'), parts along dimension 1
The draws below stay inside these ranges and needn't reach their ends.
There are 2 independent parts, one for each index of `groups`. The reference program is written for one: setup_inputs(seed, part) draws one part's arguments, and reference() takes and returns one part's arrays. A program takes and returns all parts, laid end to end along the dimension named above; each array names one. Nothing has to cross between parts.
Inputs may be any that keep to these rules, and one draw needn't show every extreme that they name: The live slots of tile t are its first counts[t] slots; some tile has all 8 live. The patch of slot j has its centre row positions[j, 0] + 128 inside tile j // 8 (object rows (j // 8) * 256 to that plus 256 - 1); its corner column lies in 0 to 256.
All inputs are finite; a program needn't handle non-finite values.
Results may differ from the reference program's by a relative error of at most 0.0003.
Values sent between devices are 32-bit elements; how exact they have to be, the bound alone decides.
A program may use at most 64 MiB of HBM per device.

```python
import math
import jax
import jax.numpy as jnp
from jax import lax

P_SIZE = 256
COLS = 512
ROWS_DEV = 256
SLOTS = 8
NR = 4096
NPOS = 128
N_ROW = 16


def draw_counts(key, part):
    key = jax.random.fold_in(key, 11)
    key_centre, key_crowded, key_sparse = jax.random.split(key, 3)
    centre = jax.random.randint(key_centre, (), 0, N_ROW)
    tiles = jnp.arange(N_ROW, dtype=jnp.int32)
    inside = (tiles - centre) % N_ROW < N_ROW // 2
    crowded = jax.random.randint(key_crowded, (N_ROW,), 3 * SLOTS // 4 + 1, SLOTS + 1)
    sparse = jax.random.randint(key_sparse, (N_ROW,), 1, SLOTS // 4 + 1)
    result = jnp.where(inside, crowded, sparse)
    return jnp.where(tiles == centre, SLOTS, result).astype(jnp.int32)


def draw_positions(key, part):
    key = jax.random.fold_in(key, 23)
    key_row, key_col = jax.random.split(key, 2)
    total_slots = N_ROW * SLOTS
    slot_tile = jnp.arange(total_slots, dtype=jnp.int32) // SLOTS
    centre_row = slot_tile * ROWS_DEV + jax.random.randint(key_row, (total_slots,), 0, ROWS_DEV)
    corner_row = centre_row - P_SIZE // 2
    corner_col = jax.random.randint(key_col, (total_slots,), 0, COLS - P_SIZE + 1)
    return jnp.stack([corner_row, corner_col], axis=1).astype(jnp.int32)


def block_levels(rng, extent, pieces, low, top_value):
    factor_of = 1.0
    for dim, parts in pieces:
        heights = jax.random.uniform(jax.random.fold_in(jax.random.fold_in(rng, 6), dim), (parts,), jnp.float32, low / len(pieces), top_value / len(pieces))
        factor_of = factor_of * jnp.repeat(jnp.exp(heights), extent[dim] // parts).reshape((-1,) + (1,) * (len(extent) - 1 - dim))
    return factor_of


def noise(stream_key, shape, spread, most, cuts=(), held_as=jnp.bfloat16):
    values = jax.random.normal(stream_key, shape, jnp.float32) * spread
    if len(cuts) > 0:
        values = block_levels(stream_key, shape, cuts, -0.22, 0.18) * values
    return jnp.clip(values, min=-most, max=most).astype(held_as)


def setup_inputs(seed: int = 0, part: int = 0) -> dict:
    arg_keys = jax.random.split(jax.random.key(seed), 6)
    part_splits = jax.random.split(jax.random.fold_in(arg_keys[5], part), 6)
    object_field = noise(part_splits[0], (2, NR, COLS), 0.7, 5.0, ((1, 16),), jnp.float32)
    probe_wave = noise(part_splits[1], (2, P_SIZE, P_SIZE), 0.7, 5.0, (), jnp.float32)
    patterns = jnp.clip(jnp.exp(math.log(4.0) - 3.6888794 * jax.random.uniform(part_splits[2], (NPOS, P_SIZE, P_SIZE), jnp.float32) ** block_levels(part_splits[2], (NPOS, P_SIZE, P_SIZE), ((0, 16),), -0.2, 0.2)), 0.1, 4.0)
    positions = draw_positions(jax.random.fold_in(jax.random.fold_in(arg_keys[5], part), 71), part)
    counts = draw_counts(jax.random.fold_in(jax.random.fold_in(arg_keys[5], part), 71), part)
    return {"object_field": object_field, "probe_wave": probe_wave, "patterns": patterns, "positions": positions, "counts": counts}


def reference(object_field, probe_wave, patterns, positions, counts):
    half_width = P_SIZE // 2
    padded = jnp.pad(object_field, ((0, 0), (half_width, half_width), (0, 0)))
    slot_ids = jnp.arange(N_ROW * SLOTS, dtype=jnp.int32)
    alive_mask = ((slot_ids % SLOTS) < counts[slot_ids // SLOTS]).astype(jnp.float32)
    probe_complex = lax.complex(probe_wave[0], probe_wave[1])
    anchor = jnp.zeros((), jnp.int32)

    def visit_slot(totals, slot_data):
        object_total, probe_total = totals
        corner, pattern, alive = slot_data
        starts = (anchor, (corner[0] + half_width).astype(jnp.int32), corner[1].astype(jnp.int32))
        patch = lax.dynamic_slice(padded, starts, (2, P_SIZE, P_SIZE))
        patch_complex = lax.complex(patch[0], patch[1])
        spectrum = jnp.fft.fft2(probe_complex * patch_complex, norm="ortho")
        misfit = (spectrum.real * spectrum.real + spectrum.imag * spectrum.imag - pattern) * alive
        gradient = jnp.fft.ifft2(misfit * spectrum, norm="ortho")
        object_part = jnp.conj(probe_complex) * gradient
        probe_part = jnp.conj(patch_complex) * gradient
        current = lax.dynamic_slice(object_total, starts, (2, P_SIZE, P_SIZE))
        object_total = lax.dynamic_update_slice(
            object_total, current + jnp.stack([object_part.real, object_part.imag]), starts)
        probe_total = probe_total + jnp.stack([probe_part.real, probe_part.imag])
        return (object_total, probe_total), None

    initial = (jnp.zeros_like(padded), jnp.zeros_like(probe_wave))
    (object_total, probe_total), unused = lax.scan(visit_slot, initial, (positions, patterns, alive_mask))
    return object_total[:, half_width:half_width + NR], probe_total
```

```python
import functools
import math

import jax
import jax.numpy as jnp
import ml_dtypes
import numpy as np
from jax import lax
from jax.experimental import pallas as pl
from jax.experimental.pallas import tpu as pltpu
from jax.sharding import PartitionSpec as P

F32 = jnp.float32
BF16 = jnp.bfloat16


def tables(extent):
    half = extent // 2
    line = np.arange(half)
    out = []
    for parity in (0, 1):
        angle = ((2 * line[:, None] + parity) * line[None, :] % extent) * (2.0 * math.pi / extent)
        cos, sin = np.cos(angle) / math.sqrt(extent), np.sin(angle) / math.sqrt(extent)
        full = np.block([[cos, sin], [-sin, cos]])
        for matrix in (full, full.T):
            high = matrix.astype(ml_dtypes.bfloat16)
            low = (matrix - high.astype(np.float64)).astype(ml_dtypes.bfloat16)
            out += [high, low]
    order = np.zeros((extent, extent), np.float32)
    order[2 * line, line] = 1
    order[2 * line + 1, half + line] = 1
    out.append(order.astype(ml_dtypes.bfloat16))
    return np.stack(out)


def parts(value):
    high = value.astype(BF16)
    return high, (value - high.astype(F32)).astype(BF16)


def dot(left, right):
    return jnp.dot(left, right, preferred_element_type=F32)


def from_left(table, index, value):
    high, low = parts(value)
    return dot(
        jnp.concatenate([table[index], table[index], table[index + 1]], axis=1),
        jnp.concatenate([high, low, high], axis=0),
    )


def from_right(value, table, index):
    high, low = parts(value)
    return dot(
        jnp.concatenate([high, low, high], axis=1),
        jnp.concatenate([table[index], table[index], table[index + 1]], axis=0),
    )


def lanes(*blocks):
    return jnp.concatenate(blocks, axis=1)


def rows(*blocks):
    return jnp.concatenate(blocks, axis=0)


def transform(re, im, table):
    h = re.shape[0] // 2
    even = from_right(lanes(re[:, :h] + re[:, h:], im[:, :h] + im[:, h:]), table, 2)
    odd = from_right(lanes(re[:, :h] - re[:, h:], im[:, :h] - im[:, h:]), table, 6)
    re, im = lanes(even[:, :h], odd[:, :h]), lanes(even[:, h:], odd[:, h:])
    even = from_left(table, 0, rows(re[:h] + re[h:], im[:h] + im[h:]))
    odd = from_left(table, 4, rows(re[:h] - re[h:], im[:h] - im[h:]))
    return even, odd


def inverse(even, odd, table):
    h = even.shape[0] // 2
    total = from_left(table, 2, even)
    other = from_left(table, 6, odd)
    top, low = total + other, total - other
    even = from_right(rows(lanes(top[:h, :h], top[h:, :h]), lanes(low[:h, :h], low[h:, :h])), table, 0)
    odd = from_right(rows(lanes(top[:h, h:], top[h:, h:]), lanes(low[:h, h:], low[h:, h:])), table, 4)
    total, other = even + odd, even - odd
    return lanes(total[:, :h], other[:, :h]), lanes(total[:, h:], other[:, h:])


def misfit_kernel(
    corner, count, low, own, high, probe, patterns, table, grad_low, grad_own, grad_high, grad_probe, field, total, ordered
):
    extent = probe.shape[1]
    h = extent // 2
    tile = own.shape[1]
    field[:, :h] = low[...]
    field[:, h : h + tile] = own[...]
    field[:, h + tile :] = high[...]
    total[...] = jnp.zeros_like(total)
    grad_probe[...] = jnp.zeros_like(grad_probe)
    column = lax.broadcasted_iota(jnp.int32, (extent, extent), 1)

    def step(slot, carry):
        first = corner[2 * slot]
        shift = corner[2 * slot + 1]
        kept = column >= shift
        sub = lax.rem(first, 8)
        base = pl.multiple_of(first - sub, 8)
        at = pl.ds(base, extent)
        after = pl.ds(pl.multiple_of(base + extent, 8), 8)
        inside = lax.broadcasted_iota(jnp.int32, (8, extent), 0) >= sub

        def patch_of(i):
            body = jnp.where(kept, field[i, at, :extent], field[i, at, extent:])
            wrap = jnp.where(kept[:8], field[i, after, :extent], field[i, after, extent:])
            return rows(jnp.where(inside, body[:8], wrap), body[8:])

        patch = [patch_of(i) for i in (0, 1)]
        turned = [
            pltpu.roll(pltpu.roll(probe[i], lax.rem(shift, extent), 1), sub, 0) for i in (0, 1)
        ]
        even, odd = transform(
            turned[0] * patch[0] - turned[1] * patch[1], turned[0] * patch[1] + turned[1] * patch[0], table
        )
        permuted = dot(lanes(*parts(patterns[slot])), rows(table[8], table[8]))
        ordered[0] = permuted[:, :h]
        ordered[1] = permuted[:, h:]
        results = []
        for parity, value in ((0, even), (1, odd)):
            pattern = lanes(ordered[0, pl.ds(parity, h, 2), :], ordered[1, pl.ds(parity, h, 2), :])
            gap = value[:h] * value[:h] + value[h:] * value[h:] - pattern
            results.append(rows(gap * value[:h], gap * value[h:]))
        re, im = inverse(results[0], results[1], table)
        zero = jnp.zeros_like(re)
        grads = (turned[0] * re + turned[1] * im, turned[0] * im - turned[1] * re)
        for i in (0, 1):
            body = rows(jnp.where(inside, grads[i][:8], zero[:8]), grads[i][8:])
            wrap = jnp.where(inside, zero[:8], grads[i][:8])
            total[i, at, :extent] += jnp.where(kept, body, zero)
            total[i, at, extent:] += jnp.where(kept, zero, body)
            total[i, after, :extent] += jnp.where(kept[:8], wrap, zero[:8])
            total[i, after, extent:] += jnp.where(kept[:8], zero[:8], wrap)
        back = lax.rem(extent - lax.rem(shift, extent), extent)
        up = lax.rem(extent - sub, extent)
        for i, value in enumerate((patch[0] * re + patch[1] * im, patch[0] * im - patch[1] * re)):
            grad_probe[i] += pltpu.roll(pltpu.roll(value, back, 1), up, 0)
        return carry

    lax.fori_loop(0, count[0], step, 0)
    grad_low[...] = total[:, :h]
    grad_own[...] = total[:, h : h + tile]
    grad_high[...] = total[:, h + tile :]


def misfit_call(corner, count, low, own, high, probe, patterns, table):
    vmem = pl.BlockSpec(memory_space=pltpu.VMEM)
    smem = pl.BlockSpec(memory_space=pltpu.SMEM)
    height = low.shape[1] + own.shape[1] + high.shape[1]
    return pl.pallas_call(
        misfit_kernel,
        out_shape=(
            jax.ShapeDtypeStruct(low.shape, F32),
            jax.ShapeDtypeStruct(own.shape, F32),
            jax.ShapeDtypeStruct(high.shape, F32),
            jax.ShapeDtypeStruct(probe.shape, F32),
        ),
        in_specs=[smem, smem] + [vmem] * 6,
        out_specs=(vmem,) * 4,
        scratch_shapes=[pltpu.VMEM((2, height, own.shape[2]), F32)] * 2
        + [pltpu.VMEM((2, probe.shape[1], probe.shape[1] // 2), F32)],
        compiler_params=pltpu.CompilerParams(vmem_limit_bytes=48 * 1024 * 1024),
        name="misfit",
    )(corner, count, low, own, high, probe, patterns, table)


def passed_along(value, axis, steps):
    count = lax.axis_size(axis)
    leading, last = (max(0, -steps), min(count, count - steps))
    return lax.ppermute(value, axis, [(source, source + steps) for source in range(leading, last)])


def local(object_field, probe_wave, patterns, positions, counts):
    tile = object_field.shape[1]
    extent = probe_wave.shape[1]
    h = extent // 2
    me = lax.axis_index("row")
    count = lax.dynamic_slice(counts, (me,), (1,))
    low = passed_along(object_field[:, tile - h :], "row", 1)
    high = passed_along(object_field[:, :h], "row", -1)
    corner = (positions - jnp.stack([me * tile - h, 0 * me])[None]).reshape(-1)
    table = jnp.asarray(tables(extent))
    grad_low, grad_own, grad_high, grad_probe = misfit_call(
        corner, count, low, object_field, high, probe_wave, patterns, table
    )
    from_below = passed_along(grad_low, "row", -1)
    from_above = passed_along(grad_high, "row", 1)
    grad_own = grad_own + jnp.concatenate([from_above, from_below], axis=1)
    return grad_own, lax.psum(grad_probe, "row")


def solution(mesh):
    placed = (
        P(None, ("groups", "row"), None),
        P(None, "groups", None),
        P(("groups", "row"), None, None),
        P(("groups", "row"), None),
        P("groups"),
    )
    return jax.shard_map(
        local,
        mesh=mesh,
        in_specs=placed,
        out_specs=(P(None, ("groups", "row"), None), P(None, "groups", None)),
        check_vma=False,
    )
```

```python
import functools
import math

import jax
import jax.numpy as jnp
import ml_dtypes
import numpy as np
from jax import lax
from jax.experimental import pallas as pl
from jax.experimental.pallas import tpu as pltpu
from jax.sharding import PartitionSpec as P

F32 = jnp.float32
BF16 = jnp.bfloat16


def tables(extent):
    half = extent // 2
    line = np.arange(half)
    out = []
    for parity in (0, 1):
        angle = ((2 * line[:, None] + parity) * line[None, :] % extent) * (2.0 * math.pi / extent)
        cos, sin = np.cos(angle) / math.sqrt(extent), np.sin(angle) / math.sqrt(extent)
        full = np.block([[cos, sin], [-sin, cos]])
        for matrix in (full, full.T):
            high = matrix.astype(ml_dtypes.bfloat16)
            low = (matrix - high.astype(np.float64)).astype(ml_dtypes.bfloat16)
            out += [high, low]
    order = np.zeros((extent, extent), np.float32)
    order[2 * line, line] = 1
    order[2 * line + 1, half + line] = 1
    out.append(order.astype(ml_dtypes.bfloat16))
    return np.stack(out)


def parts(value):
    high = value.astype(BF16)
    return high, (value - high.astype(F32)).astype(BF16)


def dot(left, right):
    return jnp.dot(left, right, preferred_element_type=F32)


def from_left(table, index, value):
    high, low = parts(value)
    return dot(
        jnp.concatenate([table[index], table[index], table[index + 1]], axis=1),
        jnp.concatenate([high, low, high], axis=0),
    )


def from_right(value, table, index):
    high, low = parts(value)
    return dot(
        jnp.concatenate([high, low, high], axis=1),
        jnp.concatenate([table[index], table[index], table[index + 1]], axis=0),
    )


def lanes(*blocks):
    return jnp.concatenate(blocks, axis=1)


def rows(*blocks):
    return jnp.concatenate(blocks, axis=0)


def transform(re, im, table):
    h = re.shape[0] // 2
    even = from_right(lanes(re[:, :h] + re[:, h:], im[:, :h] + im[:, h:]), table, 2)
    odd = from_right(lanes(re[:, :h] - re[:, h:], im[:, :h] - im[:, h:]), table, 6)
    re, im = lanes(even[:, :h], odd[:, :h]), lanes(even[:, h:], odd[:, h:])
    even = from_left(table, 0, rows(re[:h] + re[h:], im[:h] + im[h:]))
    odd = from_left(table, 4, rows(re[:h] - re[h:], im[:h] - im[h:]))
    return even, odd


def inverse(even, odd, table):
    h = even.shape[0] // 2
    total = from_left(table, 2, even)
    other = from_left(table, 6, odd)
    top, low = total + other, total - other
    even = from_right(rows(lanes(top[:h, :h], top[h:, :h]), lanes(low[:h, :h], low[h:, :h])), table, 0)
    odd = from_right(rows(lanes(top[:h, h:], top[h:, h:]), lanes(low[:h, h:], low[h:, h:])), table, 4)
    total, other = even + odd, even - odd
    return lanes(total[:, :h], other[:, :h]), lanes(total[:, h:], other[:, h:])


def misfit_kernel(
    corner, count, low, own, high, probe, patterns, table, grad_low, grad_own, grad_high, grad_probe, field, total, ordered
):
    extent = probe.shape[1]
    h = extent // 2
    tile = own.shape[1]
    field[:, h : h + tile] = own[...]
    field[:, :h] = jnp.where(count[1] > 0, low[...], jnp.zeros_like(low))
    field[:, h + tile :] = jnp.where(count[2] > 0, high[...], jnp.zeros_like(high))
    total[...] = jnp.zeros_like(total)
    grad_probe[...] = jnp.zeros_like(grad_probe)
    column = lax.broadcasted_iota(jnp.int32, (extent, extent), 1)

    def step(slot, carry):
        first = corner[2 * slot]
        shift = corner[2 * slot + 1]
        kept = column >= shift
        sub = lax.rem(first, 8)
        base = pl.multiple_of(first - sub, 8)
        at = pl.ds(base, extent)
        after = pl.ds(pl.multiple_of(base + extent, 8), 8)
        inside = lax.broadcasted_iota(jnp.int32, (8, extent), 0) >= sub

        def patch_of(i):
            body = jnp.where(kept, field[i, at, :extent], field[i, at, extent:])
            wrap = jnp.where(kept[:8], field[i, after, :extent], field[i, after, extent:])
            return rows(jnp.where(inside, body[:8], wrap), body[8:])

        patch = [patch_of(i) for i in (0, 1)]
        turned = [
            pltpu.roll(pltpu.roll(probe[i], lax.rem(shift, extent), 1), sub, 0) for i in (0, 1)
        ]
        even, odd = transform(
            turned[0] * patch[0] - turned[1] * patch[1], turned[0] * patch[1] + turned[1] * patch[0], table
        )
        permuted = dot(lanes(*parts(patterns[slot])), rows(table[8], table[8]))
        ordered[0] = permuted[:, :h]
        ordered[1] = permuted[:, h:]
        results = []
        for parity, value in ((0, even), (1, odd)):
            pattern = lanes(ordered[0, pl.ds(parity, h, 2), :], ordered[1, pl.ds(parity, h, 2), :])
            gap = value[:h] * value[:h] + value[h:] * value[h:] - pattern
            results.append(rows(gap * value[:h], gap * value[h:]))
        re, im = inverse(results[0], results[1], table)
        zero = jnp.zeros_like(re)
        grads = (turned[0] * re + turned[1] * im, turned[0] * im - turned[1] * re)
        for i in (0, 1):
            body = rows(jnp.where(inside, grads[i][:8], zero[:8]), grads[i][8:])
            wrap = jnp.where(inside, zero[:8], grads[i][:8])
            total[i, at, :extent] += jnp.where(kept, body, zero)
            total[i, at, extent:] += jnp.where(kept, zero, body)
            total[i, after, :extent] += jnp.where(kept[:8], wrap, zero[:8])
            total[i, after, extent:] += jnp.where(kept[:8], zero[:8], wrap)
        back = lax.rem(extent - lax.rem(shift, extent), extent)
        up = lax.rem(extent - sub, extent)
        for i, value in enumerate((patch[0] * re + patch[1] * im, patch[0] * im - patch[1] * re)):
            grad_probe[i] += pltpu.roll(pltpu.roll(value, back, 1), up, 0)
        return carry

    lax.fori_loop(0, count[0], step, 0)
    grad_low[...] = total[:, :h]
    grad_own[...] = total[:, h : h + tile]
    grad_high[...] = total[:, h + tile :]


def misfit_call(corner, count, low, own, high, probe, patterns, table):
    vmem = pl.BlockSpec(memory_space=pltpu.VMEM)
    smem = pl.BlockSpec(memory_space=pltpu.SMEM)
    height = low.shape[1] + own.shape[1] + high.shape[1]
    return pl.pallas_call(
        misfit_kernel,
        out_shape=(
            jax.ShapeDtypeStruct(low.shape, F32),
            jax.ShapeDtypeStruct(own.shape, F32),
            jax.ShapeDtypeStruct(high.shape, F32),
            jax.ShapeDtypeStruct(probe.shape, F32),
        ),
        in_specs=[smem, smem] + [vmem] * 6,
        out_specs=(vmem,) * 4,
        scratch_shapes=[pltpu.VMEM((2, height, own.shape[2]), F32)] * 2
        + [pltpu.VMEM((2, probe.shape[1], probe.shape[1] // 2), F32)],
        compiler_params=pltpu.CompilerParams(vmem_limit_bytes=48 * 1024 * 1024),
        name="misfit",
    )(corner, count, low, own, high, probe, patterns, table)


def radices(count):
    out = []
    while count > 1:
        out.append(4 if len(out) >= 2 and count % 4 == 0 else 2)
        count //= out[-1]
    return out


def signal(peer):
    pl.semaphore_signal(
        pltpu.get_barrier_semaphore(), inc=1, device_id={"row": peer}, device_id_type=pl.DeviceIdType.MESH
    )


def remote(source, target, send, recv, peer):
    return pltpu.make_async_remote_copy(
        src_ref=source,
        dst_ref=target,
        send_sem=send,
        recv_sem=recv,
        device_id={"row": peer},
        device_id_type=pl.DeviceIdType.MESH,
    )


def both_sides(me, count, action):
    @pl.when(me > 0)
    def _():
        action(0)

    @pl.when(me < count - 1)
    def _():
        action(1)


def neighbours(me, count):
    return lax.min(me, 1) + lax.min(count - 1 - me, 1)


def border_kernel(count, own, low, high, send, recv):
    me = lax.axis_index("row")
    h = low.shape[1]
    up, down = lax.max(me - 1, 0), lax.min(me + 1, count - 1)
    copies = (
        remote(own.at[:, :h], high, send.at[0], recv.at[1], up),
        remote(own.at[:, own.shape[1] - h :], low, send.at[1], recv.at[0], down),
    )
    arrivals = (
        remote(own.at[:, :h], low, send.at[0], recv.at[0], up),
        remote(own.at[:, :h], high, send.at[1], recv.at[1], down),
    )
    both_sides(me, count, lambda side: signal((up, down)[side]))
    pl.semaphore_wait(pltpu.get_barrier_semaphore(), neighbours(me, count))
    both_sides(me, count, lambda side: copies[side].start())
    both_sides(me, count, lambda side: arrivals[side].wait_recv())
    both_sides(me, count, lambda side: copies[side].wait_send())


def border_call(own, h, count):
    anywhere = pl.BlockSpec(memory_space=pl.ANY)
    side = jax.ShapeDtypeStruct((own.shape[0], h, own.shape[2]), F32)
    return pl.pallas_call(
        functools.partial(border_kernel, count),
        out_shape=(side, side),
        in_specs=[anywhere],
        out_specs=(anywhere, anywhere),
        scratch_shapes=[pltpu.SemaphoreType.DMA((2,)), pltpu.SemaphoreType.DMA((2,))],
        compiler_params=pltpu.CompilerParams(collective_id=0, has_side_effects=True),
        name="border",
    )(own)


def sums_kernel(count, grad_low, grad_own, grad_high, probe, out, out_probe, from_above, from_below, *scratch):
    me = lax.axis_index("row")
    h = grad_low.shape[1]
    tile = grad_own.shape[1]
    steps = radices(count)
    halo_send, halo_recv, rs_send, rs_recv, ag_send, ag_recv = scratch[:6]
    held = scratch[6 : 6 + len(steps)]
    landed = scratch[6 + len(steps) :]
    up, down = lax.max(me - 1, 0), lax.min(me + 1, count - 1)

    levels = []
    stride, size, start = 1, probe.shape[0], 0
    index = 0
    for radix in steps:
        digit = lax.rem(me // stride, radix)
        size //= radix
        others = []
        for k in range(1, radix):
            other = lax.rem(digit + k, radix)
            others.append((index, k, other, me + (other - digit) * stride))
            index += 1
        levels.append((radix, digit, size, start, others))
        start = start + digit * size
        stride *= radix

    both_sides(me, count, lambda side: signal((up, down)[side]))
    for level in levels:
        for _, _, _, peer in level[4]:
            signal(peer)
    pl.semaphore_wait(pltpu.get_barrier_semaphore(), index + neighbours(me, count))

    halos = (
        remote(grad_low, from_below, halo_send.at[0], halo_recv.at[1], up),
        remote(grad_high, from_above, halo_send.at[1], halo_recv.at[0], down),
    )
    arrivals = (
        remote(grad_low, from_above, halo_send.at[0], halo_recv.at[0], up),
        remote(grad_high, from_below, halo_send.at[1], halo_recv.at[1], down),
    )

    def rs_copies(depth):
        radix, digit, size, _, others = levels[depth]
        source = probe if depth == 0 else held[depth - 1]
        return [
            remote(
                source.at[pl.ds(pl.multiple_of(other * size, 8), size)],
                landed[depth].at[radix - 1 - k],
                rs_send.at[i],
                rs_recv.at[levels[depth][4][radix - 1 - k][0]],
                peer,
            )
            for i, k, other, peer in others
        ]

    def rs_arrivals(depth):
        radix, digit, size, _, others = levels[depth]
        source = probe if depth == 0 else held[depth - 1]
        return [
            remote(source.at[pl.ds(0, size)], landed[depth].at[k - 1], rs_send.at[i], rs_recv.at[i], peer)
            for i, k, other, peer in others
        ]

    started = []
    for depth, (radix, digit, size, _, others) in enumerate(levels):
        copies = rs_copies(depth)
        for copy in copies:
            copy.start()
        started += copies
        if depth == 0:
            both_sides(me, count, lambda side: halos[side].start())
        source = probe if depth == 0 else held[depth - 1]
        value = source[pl.ds(pl.multiple_of(digit * size, 8), size)]
        for k, arrival in enumerate(rs_arrivals(depth)):
            arrival.wait_recv()
            value = value + landed[depth][k]
        held[depth][...] = value

    mine = pl.ds(pl.multiple_of(start, 8), levels[-1][2])
    out_probe[mine] = held[-1][...]
    for depth in reversed(range(len(levels))):
        radix, digit, size, first, others = levels[depth]
        region = pl.ds(pl.multiple_of(first + digit * size, 8), size)
        copies = [
            remote(
                out_probe.at[region],
                out_probe.at[region],
                ag_send.at[i],
                ag_recv.at[others[radix - 1 - k][0]],
                peer,
            )
            for i, k, other, peer in others
        ]
        for copy in copies:
            copy.start()
        started += copies
        for i, k, other, peer in others:
            theirs = pl.ds(pl.multiple_of(first + other * size, 8), size)
            remote(out_probe.at[region], out_probe.at[theirs], ag_send.at[i], ag_recv.at[i], peer).wait_recv()

    out[...] = grad_own[...]

    def add_side(side):
        arrivals[side].wait_recv()
        where, value = ((slice(0, h), from_above), (slice(tile - h, tile), from_below))[side]
        out[:, where] += value[...]

    both_sides(me, count, add_side)
    for copy in started:
        copy.wait_send()
    both_sides(me, count, lambda side: halos[side].wait_send())


def sums_call(grad_low, grad_own, grad_high, probe, count):
    vmem = pl.BlockSpec(memory_space=pltpu.VMEM)
    steps = radices(count)
    pieces = sum(radix - 1 for radix in steps)
    held, landed, size = [], [], probe.shape[0]
    for radix in steps:
        size //= radix
        held.append(pltpu.VMEM((size, probe.shape[1]), F32))
        landed.append(pltpu.VMEM((radix - 1, size, probe.shape[1]), F32))
    return pl.pallas_call(
        functools.partial(sums_kernel, count),
        out_shape=(jax.ShapeDtypeStruct(grad_own.shape, F32), jax.ShapeDtypeStruct(probe.shape, F32)),
        in_specs=[vmem] * 4,
        out_specs=(vmem, vmem),
        scratch_shapes=[pltpu.VMEM(grad_low.shape, F32)] * 2
        + [pltpu.SemaphoreType.DMA((2,))] * 2
        + [pltpu.SemaphoreType.DMA((pieces,))] * 4
        + held
        + landed,
        compiler_params=pltpu.CompilerParams(
            collective_id=1, has_side_effects=True, vmem_limit_bytes=40 * 1024 * 1024
        ),
        name="sums",
    )(grad_low, grad_own, grad_high, probe)


def local(object_field, probe_wave, patterns, positions, counts):
    tile = object_field.shape[1]
    extent = probe_wave.shape[1]
    h = extent // 2
    me = lax.axis_index("row")
    size = lax.axis_size("row")
    count = lax.dynamic_slice(counts, (me,), (1,))
    low, high = border_call(object_field, h, size)
    corner = (positions - jnp.stack([me * tile - h, 0 * me])[None]).reshape(-1)
    setup = jnp.concatenate([count, jnp.stack([me > 0, me < size - 1]).astype(jnp.int32)])
    table = jnp.asarray(tables(extent))
    grad_low, grad_own, grad_high, grad_probe = misfit_call(
        corner, setup, low, object_field, high, probe_wave, patterns, table
    )
    grads, total = sums_call(grad_low, grad_own, grad_high, grad_probe.reshape(-1, extent), size)
    return grads, total.reshape(grad_probe.shape)


def solution(mesh):
    placed = (
        P(None, ("groups", "row"), None),
        P(None, "groups", None),
        P(("groups", "row"), None, None),
        P(("groups", "row"), None),
        P("groups"),
    )
    return jax.shard_map(
        local,
        mesh=mesh,
        in_specs=placed,
        out_specs=(P(None, ("groups", "row"), None), P(None, "groups", None)),
        check_vma=False,
    )
```

```python
import functools
import math

import jax
import jax.numpy as jnp
import ml_dtypes
import numpy as np
from jax import lax
from jax.experimental import pallas as pl
from jax.experimental.pallas import tpu as pltpu
from jax.sharding import PartitionSpec as P

F32 = jnp.float32
BF16 = jnp.bfloat16
WIDTH = 2


def tables(extent):
    half = extent // 2
    line = np.arange(half)
    out = []
    for parity in (0, 1):
        angle = ((2 * line[:, None] + parity) * line[None, :] % extent) * (2.0 * math.pi / extent)
        cos, sin = np.cos(angle) / math.sqrt(extent), np.sin(angle) / math.sqrt(extent)
        full = np.block([[cos, sin], [-sin, cos]])
        for matrix in (full, full.T):
            high = matrix.astype(ml_dtypes.bfloat16)
            low = (matrix - high.astype(np.float64)).astype(ml_dtypes.bfloat16)
            out += [high, low]
    order = np.zeros((extent, extent), np.float32)
    order[2 * line, line] = 1
    order[2 * line + 1, half + line] = 1
    out.append(order.astype(ml_dtypes.bfloat16))
    return np.stack(out)


def parts(value):
    high = value.astype(BF16)
    return high, (value - high.astype(F32)).astype(BF16)


def dot(left, right):
    return jnp.dot(left, right, preferred_element_type=F32)


def from_left(table, index, value):
    high, low = parts(value)
    return dot(
        jnp.concatenate([table[index], table[index], table[index + 1]], axis=1),
        jnp.concatenate([high, low, high], axis=0),
    )


def from_right(value, table, index):
    high, low = parts(value)
    return dot(
        jnp.concatenate([high, low, high], axis=1),
        jnp.concatenate([table[index], table[index], table[index + 1]], axis=0),
    )


def lanes(*blocks):
    return jnp.concatenate(blocks, axis=1)


def rows(*blocks):
    return jnp.concatenate(blocks, axis=0)


def transform(re, im, table):
    h = re.shape[0] // 2
    even = from_right(lanes(re[:, :h] + re[:, h:], im[:, :h] + im[:, h:]), table, 2)
    odd = from_right(lanes(re[:, :h] - re[:, h:], im[:, :h] - im[:, h:]), table, 6)
    re, im = lanes(even[:, :h], odd[:, :h]), lanes(even[:, h:], odd[:, h:])
    even = from_left(table, 0, rows(re[:h] + re[h:], im[:h] + im[h:]))
    odd = from_left(table, 4, rows(re[:h] - re[h:], im[:h] - im[h:]))
    return even, odd


def inverse(even, odd, table):
    h = even.shape[0] // 2
    total = from_left(table, 2, even)
    other = from_left(table, 6, odd)
    top, low = total + other, total - other
    even = from_right(rows(lanes(top[:h, :h], top[h:, :h]), lanes(low[:h, :h], low[h:, :h])), table, 0)
    odd = from_right(rows(lanes(top[:h, h:], top[h:, h:]), lanes(low[:h, h:], low[h:, h:])), table, 4)
    total, other = even + odd, even - odd
    return lanes(total[:, :h], other[:, :h]), lanes(total[:, h:], other[:, h:])


def misfit_kernel(positions, counts, field, probe, patterns, table, total, grad_probe, ordered):
    extent = probe.shape[1]
    h = extent // 2
    tile = field.shape[1] - extent
    me = lax.axis_index("row")
    live = counts[me]
    total[...] = jnp.zeros_like(total)
    grad_probe[...] = jnp.zeros_like(grad_probe)
    column = lax.broadcasted_iota(jnp.int32, (extent, extent), 1)

    def load(slot):
        first = positions[slot, 0] - (me * tile - h)
        shift = positions[slot, 1]
        kept = column >= shift
        sub = lax.rem(first, 8)
        base = pl.multiple_of(first - sub, 8)
        at = pl.ds(base, extent)
        after = pl.ds(pl.multiple_of(base + extent, 8), 8)
        inside = lax.broadcasted_iota(jnp.int32, (8, extent), 0) >= sub

        def patch_of(i):
            body = jnp.where(kept, field[i, at, :extent], field[i, at, extent:])
            wrap = jnp.where(kept[:8], field[i, after, :extent], field[i, after, extent:])
            return rows(jnp.where(inside, body[:8], wrap), body[8:])

        patch = [patch_of(i) for i in (0, 1)]
        turned = [
            pltpu.roll(pltpu.roll(probe[i], lax.rem(shift, extent), 1), sub, 0) for i in (0, 1)
        ]
        return shift, kept, sub, at, after, inside, patch, turned

    def gradient(slot, lane, patch, turned):
        even, odd = transform(
            turned[0] * patch[0] - turned[1] * patch[1], turned[0] * patch[1] + turned[1] * patch[0], table
        )
        permuted = dot(lanes(*parts(patterns[slot])), rows(table[8], table[8]))
        ordered[lane, 0] = permuted[:, :h]
        ordered[lane, 1] = permuted[:, h:]
        alive = (slot < live).astype(F32)
        results = []
        for parity, value in ((0, even), (1, odd)):
            picked = pl.ds(parity, h, 2)
            pattern = lanes(ordered[lane, 0, picked, :], ordered[lane, 1, picked, :])
            gap = (value[:h] * value[:h] + value[h:] * value[h:] - pattern) * alive
            results.append(rows(gap * value[:h], gap * value[h:]))
        return inverse(results[0], results[1], table)

    def add(where, patch, turned, re, im):
        shift, kept, sub, at, after, inside = where
        zero = jnp.zeros_like(re)
        grads = (turned[0] * re + turned[1] * im, turned[0] * im - turned[1] * re)
        for i in (0, 1):
            body = rows(jnp.where(inside, grads[i][:8], zero[:8]), grads[i][8:])
            wrap = jnp.where(inside, zero[:8], grads[i][:8])
            total[i, at, :extent] += jnp.where(kept, body, zero)
            total[i, at, extent:] += jnp.where(kept, zero, body)
            total[i, after, :extent] += jnp.where(kept[:8], wrap, zero[:8])
            total[i, after, extent:] += jnp.where(kept[:8], zero[:8], wrap)
        back = lax.rem(extent - lax.rem(shift, extent), extent)
        up = lax.rem(extent - sub, extent)
        for i, value in enumerate((patch[0] * re + patch[1] * im, patch[0] * im - patch[1] * re)):
            grad_probe[i] += pltpu.roll(pltpu.roll(value, back, 1), up, 0)

    def step(group, carry):
        slots = [group * WIDTH + lane for lane in range(WIDTH)]
        loaded = [load(slot) for slot in slots]
        grads = [gradient(slot, lane, *loaded[lane][6:]) for lane, slot in enumerate(slots)]
        for one, (re, im) in zip(loaded, grads):
            add(one[:6], one[6], one[7], re, im)
        return carry

    lax.fori_loop(0, (live + WIDTH - 1) // WIDTH, step, 0)


def misfit_call(positions, counts, field, probe, patterns, table):
    vmem = pl.BlockSpec(memory_space=pltpu.VMEM)
    smem = pl.BlockSpec(memory_space=pltpu.SMEM)
    return pl.pallas_call(
        misfit_kernel,
        out_shape=(jax.ShapeDtypeStruct(field.shape, F32), jax.ShapeDtypeStruct(probe.shape, F32)),
        in_specs=[smem, smem] + [vmem] * 4,
        out_specs=(vmem, vmem),
        scratch_shapes=[pltpu.VMEM((WIDTH, 2, probe.shape[1], probe.shape[1] // 2), F32)],
        compiler_params=pltpu.CompilerParams(vmem_limit_bytes=44 * 1024 * 1024),
        name="misfit",
    )(positions, counts, field, probe, patterns, table)


def radices(count):
    out = []
    while count > 1:
        out.append(4 if len(out) >= 2 and count % 4 == 0 else 2)
        count //= out[-1]
    return out


def signal(peer):
    pl.semaphore_signal(
        pltpu.get_barrier_semaphore(), inc=1, device_id={"row": peer}, device_id_type=pl.DeviceIdType.MESH
    )


def remote(source, target, send, recv, peer):
    return pltpu.make_async_remote_copy(
        src_ref=source,
        dst_ref=target,
        send_sem=send,
        recv_sem=recv,
        device_id={"row": peer},
        device_id_type=pl.DeviceIdType.MESH,
    )


def both_sides(me, count, action):
    @pl.when(me > 0)
    def _():
        action(0)

    @pl.when(me < count - 1)
    def _():
        action(1)


def neighbours(me, count):
    return lax.min(me, 1) + lax.min(count - 1 - me, 1)


def border_kernel(count, own, probe, patterns, table, field, probe_in, patterns_in, table_in, send, recv, here):
    me = lax.axis_index("row")
    tile = own.shape[1]
    h = (field.shape[1] - tile) // 2
    up, down = lax.max(me - 1, 0), lax.min(me + 1, count - 1)
    low, high = field.at[:, :h], field.at[:, h + tile :]
    moves = [
        pltpu.make_async_copy(source, target, here.at[i])
        for i, (source, target) in enumerate(
            (
                (own, field.at[:, h : h + tile]),
                (probe, probe_in),
                (patterns, patterns_in),
                (table, table_in),
            )
        )
    ]
    copies = (
        remote(own.at[:, :h], high, send.at[0], recv.at[1], up),
        remote(own.at[:, tile - h :], low, send.at[1], recv.at[0], down),
    )
    arrivals = (
        remote(own.at[:, :h], low, send.at[0], recv.at[0], up),
        remote(own.at[:, :h], high, send.at[1], recv.at[1], down),
    )
    both_sides(me, count, lambda side: signal((up, down)[side]))
    pl.semaphore_wait(pltpu.get_barrier_semaphore(), neighbours(me, count))
    both_sides(me, count, lambda side: copies[side].start())
    for move in moves:
        move.start()

    @pl.when(me == 0)
    def _():
        field[:, :h] = jnp.zeros((2, h, field.shape[2]), F32)

    @pl.when(me == count - 1)
    def _():
        field[:, h + tile :] = jnp.zeros((2, h, field.shape[2]), F32)

    for move in moves:
        move.wait()
    both_sides(me, count, lambda side: arrivals[side].wait_recv())
    both_sides(me, count, lambda side: copies[side].wait_send())


def border_call(own, probe, patterns, table, h, count):
    anywhere = pl.BlockSpec(memory_space=pl.ANY)
    vmem = pl.BlockSpec(memory_space=pltpu.VMEM)
    field = jax.ShapeDtypeStruct((own.shape[0], own.shape[1] + 2 * h, own.shape[2]), F32)
    same = [jax.ShapeDtypeStruct(value.shape, value.dtype) for value in (probe, patterns, table)]
    return pl.pallas_call(
        functools.partial(border_kernel, count),
        out_shape=(field, *same),
        in_specs=[anywhere] * 4,
        out_specs=(vmem,) * 4,
        scratch_shapes=[pltpu.SemaphoreType.DMA((2,)), pltpu.SemaphoreType.DMA((2,)), pltpu.SemaphoreType.DMA((4,))],
        compiler_params=pltpu.CompilerParams(
            collective_id=0, has_side_effects=True, vmem_limit_bytes=40 * 1024 * 1024
        ),
        name="border",
    )(own, probe, patterns, table)


def sums_kernel(count, grads, probe, out, out_probe, from_above, from_below, *scratch):
    me = lax.axis_index("row")
    tile = out.shape[1]
    h = from_above.shape[1]
    grad_low, grad_high = grads.at[:, :h], grads.at[:, h + tile :]
    steps = radices(count)
    halo_send, halo_recv, rs_send, rs_recv, ag_send, ag_recv = scratch[:6]
    held = scratch[6 : 6 + len(steps)]
    landed = scratch[6 + len(steps) :]
    up, down = lax.max(me - 1, 0), lax.min(me + 1, count - 1)

    levels = []
    stride, size, start = 1, probe.shape[0], 0
    index = 0
    for radix in steps:
        digit = lax.rem(me // stride, radix)
        size //= radix
        others = []
        for k in range(1, radix):
            other = lax.rem(digit + k, radix)
            others.append((index, k, other, me + (other - digit) * stride))
            index += 1
        levels.append((radix, digit, size, start, others))
        start = start + digit * size
        stride *= radix

    both_sides(me, count, lambda side: signal((up, down)[side]))
    for level in levels:
        for _, _, _, peer in level[4]:
            signal(peer)
    pl.semaphore_wait(pltpu.get_barrier_semaphore(), index + neighbours(me, count))

    halos = (
        remote(grad_low, from_below, halo_send.at[0], halo_recv.at[1], up),
        remote(grad_high, from_above, halo_send.at[1], halo_recv.at[0], down),
    )
    arrivals = (
        remote(grad_low, from_above, halo_send.at[0], halo_recv.at[0], up),
        remote(grad_high, from_below, halo_send.at[1], halo_recv.at[1], down),
    )

    def rs_copies(depth):
        radix, digit, size, _, others = levels[depth]
        source = probe if depth == 0 else held[depth - 1]
        return [
            remote(
                source.at[pl.ds(pl.multiple_of(other * size, 8), size)],
                landed[depth].at[radix - 1 - k],
                rs_send.at[i],
                rs_recv.at[levels[depth][4][radix - 1 - k][0]],
                peer,
            )
            for i, k, other, peer in others
        ]

    def rs_arrivals(depth):
        radix, digit, size, _, others = levels[depth]
        source = probe if depth == 0 else held[depth - 1]
        return [
            remote(source.at[pl.ds(0, size)], landed[depth].at[k - 1], rs_send.at[i], rs_recv.at[i], peer)
            for i, k, other, peer in others
        ]

    started = []
    for depth, (radix, digit, size, _, others) in enumerate(levels):
        copies = rs_copies(depth)
        for copy in copies:
            copy.start()
        started += copies
        if depth == min(1, len(levels) - 1):
            both_sides(me, count, lambda side: halos[side].start())
        source = probe if depth == 0 else held[depth - 1]
        value = source[pl.ds(pl.multiple_of(digit * size, 8), size)]
        for k, arrival in enumerate(rs_arrivals(depth)):
            arrival.wait_recv()
            value = value + landed[depth][k]
        held[depth][...] = value

    mine = pl.ds(pl.multiple_of(start, 8), levels[-1][2])
    out_probe[mine] = held[-1][...]
    for depth in reversed(range(len(levels))):
        radix, digit, size, first, others = levels[depth]
        region = pl.ds(pl.multiple_of(first + digit * size, 8), size)
        copies = [
            remote(
                out_probe.at[region],
                out_probe.at[region],
                ag_send.at[i],
                ag_recv.at[others[radix - 1 - k][0]],
                peer,
            )
            for i, k, other, peer in others
        ]
        for copy in copies:
            copy.start()
        started += copies
        for i, k, other, peer in others:
            theirs = pl.ds(pl.multiple_of(first + other * size, 8), size)
            remote(out_probe.at[region], out_probe.at[theirs], ag_send.at[i], ag_recv.at[i], peer).wait_recv()

    out[...] = grads[:, h : h + tile]

    def add_side(side):
        arrivals[side].wait_recv()
        where, value = ((slice(0, h), from_above), (slice(tile - h, tile), from_below))[side]
        out[:, where] += value[...]

    both_sides(me, count, add_side)
    for copy in started:
        copy.wait_send()
    both_sides(me, count, lambda side: halos[side].wait_send())


def sums_call(grads, probe, h, count):
    vmem = pl.BlockSpec(memory_space=pltpu.VMEM)
    steps = radices(count)
    pieces = sum(radix - 1 for radix in steps)
    held, landed, size = [], [], probe.shape[0]
    for radix in steps:
        size //= radix
        held.append(pltpu.VMEM((size, probe.shape[1]), F32))
        landed.append(pltpu.VMEM((radix - 1, size, probe.shape[1]), F32))
    return pl.pallas_call(
        functools.partial(sums_kernel, count),
        out_shape=(jax.ShapeDtypeStruct((grads.shape[0], grads.shape[1] - 2 * h, grads.shape[2]), F32), jax.ShapeDtypeStruct(probe.shape, F32)),
        in_specs=[vmem] * 2,
        out_specs=(vmem, vmem),
        scratch_shapes=[pltpu.VMEM((grads.shape[0], h, grads.shape[2]), F32)] * 2
        + [pltpu.SemaphoreType.DMA((2,))] * 2
        + [pltpu.SemaphoreType.DMA((pieces,))] * 4
        + held
        + landed,
        compiler_params=pltpu.CompilerParams(
            collective_id=1, has_side_effects=True, vmem_limit_bytes=40 * 1024 * 1024
        ),
        name="sums",
    )(grads, probe)


def local(object_field, probe_wave, patterns, positions, counts):
    extent = probe_wave.shape[1]
    h = extent // 2
    size = lax.axis_size("row")
    table = jnp.asarray(tables(extent))
    field, probe, patterns, table = border_call(object_field, probe_wave, patterns, table, h, size)
    grads, grad_probe = misfit_call(positions, counts, field, probe, patterns, table)
    grads, grad_probe = sums_call(grads, grad_probe.reshape(-1, extent), h, size)
    return grads, grad_probe.reshape(probe_wave.shape)


def solution(mesh):
    placed = (
        P(None, ("groups", "row"), None),
        P(None, "groups", None),
        P(("groups", "row"), None, None),
        P(("groups", "row"), None),
        P("groups"),
    )
    return jax.shard_map(
        local,
        mesh=mesh,
        in_specs=placed,
        out_specs=(P(None, ("groups", "row"), None), P(None, "groups", None)),
        check_vma=False,
    )
```

```python
import functools
import math

import jax
import jax.numpy as jnp
import ml_dtypes
import numpy as np
from jax import lax
from jax.experimental import pallas as pl
from jax.experimental.pallas import tpu as pltpu
from jax.sharding import PartitionSpec as P

F32 = jnp.float32
BF16 = jnp.bfloat16
WIDTH = 2


def tables(extent):
    half = extent // 2
    line = np.arange(half)
    out = []
    for parity in (0, 1):
        angle = ((2 * line[:, None] + parity) * line[None, :] % extent) * (2.0 * math.pi / extent)
        cos, sin = np.cos(angle) / math.sqrt(extent), np.sin(angle) / math.sqrt(extent)
        full = np.block([[cos, sin], [-sin, cos]])
        for matrix in (full, full.T):
            high = matrix.astype(ml_dtypes.bfloat16)
            low = (matrix - high.astype(np.float64)).astype(ml_dtypes.bfloat16)
            out += [high, low]
    order = np.zeros((extent, extent), np.float32)
    order[2 * line, line] = 1
    order[2 * line + 1, half + line] = 1
    out.append(order.astype(ml_dtypes.bfloat16))
    return np.stack(out)


def parts(value):
    high = value.astype(BF16)
    return high, (value - high.astype(F32)).astype(BF16)


def dot(left, right):
    return jnp.dot(left, right, preferred_element_type=F32)


def from_left(table, index, value):
    high, low = parts(value)
    return dot(
        jnp.concatenate([table[index], table[index], table[index + 1]], axis=1),
        jnp.concatenate([high, low, high], axis=0),
    )


def from_right(value, table, index):
    high, low = parts(value)
    return dot(
        jnp.concatenate([high, low, high], axis=1),
        jnp.concatenate([table[index], table[index], table[index + 1]], axis=0),
    )


def lanes(*blocks):
    return jnp.concatenate(blocks, axis=1)


def rows(*blocks):
    return jnp.concatenate(blocks, axis=0)


def transform(re, im, table):
    h = re.shape[0] // 2
    even = from_right(lanes(re[:, :h] + re[:, h:], im[:, :h] + im[:, h:]), table, 2)
    odd = from_right(lanes(re[:, :h] - re[:, h:], im[:, :h] - im[:, h:]), table, 6)
    re, im = lanes(even[:, :h], odd[:, :h]), lanes(even[:, h:], odd[:, h:])
    even = from_left(table, 0, rows(re[:h] + re[h:], im[:h] + im[h:]))
    odd = from_left(table, 4, rows(re[:h] - re[h:], im[:h] - im[h:]))
    return even, odd


def inverse(even, odd, table):
    h = even.shape[0] // 2
    total = from_left(table, 2, even)
    other = from_left(table, 6, odd)
    top, low = total + other, total - other
    even = from_right(rows(lanes(top[:h, :h], top[h:, :h]), lanes(low[:h, :h], low[h:, :h])), table, 0)
    odd = from_right(rows(lanes(top[:h, h:], top[h:, h:]), lanes(low[:h, h:], low[h:, h:])), table, 4)
    total, other = even + odd, even - odd
    return lanes(total[:, :h], other[:, :h]), lanes(total[:, h:], other[:, h:])


def turned_rows(value, amount, up):
    groups = value.reshape(value.shape[0] // 8, 8, value.shape[1])
    place = lax.broadcasted_iota(jnp.int32, groups.shape, 1)
    if up:
        inner = pltpu.roll(groups, lax.rem(8 - amount, 8), 1)
        other = jnp.concatenate([inner[1:], inner[:1]], axis=0)
        result = jnp.where(place < 8 - amount, inner, other)
    else:
        inner = pltpu.roll(groups, amount, 1)
        other = jnp.concatenate([inner[-1:], inner[:-1]], axis=0)
        result = jnp.where(place >= amount, inner, other)
    return result.reshape(value.shape)


def misfit_kernel(positions, counts, field, probe, patterns, table, total, grad_probe, ordered):
    extent = probe.shape[1]
    h = extent // 2
    tile = field.shape[1] - extent
    me = lax.axis_index("row")
    live = counts[me]
    total[...] = jnp.zeros_like(total)
    grad_probe[...] = jnp.zeros_like(grad_probe)
    column = lax.broadcasted_iota(jnp.int32, (extent, extent), 1)

    def load(slot):
        first = positions[slot, 0] - (me * tile - h)
        shift = positions[slot, 1]
        kept = column >= shift
        sub = lax.rem(first, 8)
        base = pl.multiple_of(first - sub, 8)
        at = pl.ds(base, extent)
        after = pl.ds(pl.multiple_of(base + extent, 8), 8)
        inside = lax.broadcasted_iota(jnp.int32, (8, extent), 0) >= sub

        def patch_of(i):
            body = jnp.where(kept, field[i, at, :extent], field[i, at, extent:])
            wrap = jnp.where(kept[:8], field[i, after, :extent], field[i, after, extent:])
            return rows(jnp.where(inside, body[:8], wrap), body[8:])

        patch = [patch_of(i) for i in (0, 1)]
        turned = [
            turned_rows(pltpu.roll(probe[i], lax.rem(shift, extent), 1), sub, False) for i in (0, 1)
        ]
        return shift, kept, sub, at, after, inside, patch, turned

    def gradient(slot, lane, patch, turned):
        even, odd = transform(
            turned[0] * patch[0] - turned[1] * patch[1], turned[0] * patch[1] + turned[1] * patch[0], table
        )
        permuted = dot(lanes(*parts(patterns[slot])), rows(table[8], table[8]))
        ordered[lane, 0] = permuted[:, :h]
        ordered[lane, 1] = permuted[:, h:]
        alive = (slot < live).astype(F32)
        results = []
        for parity, value in ((0, even), (1, odd)):
            picked = pl.ds(parity, h, 2)
            pattern = lanes(ordered[lane, 0, picked, :], ordered[lane, 1, picked, :])
            gap = (value[:h] * value[:h] + value[h:] * value[h:] - pattern) * alive
            results.append(rows(gap * value[:h], gap * value[h:]))
        return inverse(results[0], results[1], table)

    def add(where, patch, turned, re, im):
        shift, kept, sub, at, after, inside = where
        zero = jnp.zeros_like(re)
        grads = (turned[0] * re + turned[1] * im, turned[0] * im - turned[1] * re)
        for i in (0, 1):
            body = rows(jnp.where(inside, grads[i][:8], zero[:8]), grads[i][8:])
            wrap = jnp.where(inside, zero[:8], grads[i][:8])
            total[i, at, :extent] += jnp.where(kept, body, zero)
            total[i, at, extent:] += jnp.where(kept, zero, body)
            total[i, after, :extent] += jnp.where(kept[:8], wrap, zero[:8])
            total[i, after, extent:] += jnp.where(kept[:8], zero[:8], wrap)
        back = lax.rem(extent - lax.rem(shift, extent), extent)
        for i, value in enumerate((patch[0] * re + patch[1] * im, patch[0] * im - patch[1] * re)):
            grad_probe[i] += turned_rows(pltpu.roll(value, back, 1), sub, True)

    def step(group, carry):
        slots = [group * WIDTH + lane for lane in range(WIDTH)]
        loaded = [load(slot) for slot in slots]
        grads = [gradient(slot, lane, *loaded[lane][6:]) for lane, slot in enumerate(slots)]
        for one, (re, im) in zip(loaded, grads):
            add(one[:6], one[6], one[7], re, im)
        return carry

    lax.fori_loop(0, (live + WIDTH - 1) // WIDTH, step, 0)


def misfit_call(positions, counts, field, probe, patterns, table):
    vmem = pl.BlockSpec(memory_space=pltpu.VMEM)
    smem = pl.BlockSpec(memory_space=pltpu.SMEM)
    return pl.pallas_call(
        misfit_kernel,
        out_shape=(jax.ShapeDtypeStruct(field.shape, F32), jax.ShapeDtypeStruct(probe.shape, F32)),
        in_specs=[smem, smem] + [vmem] * 4,
        out_specs=(vmem, vmem),
        scratch_shapes=[pltpu.VMEM((WIDTH, 2, probe.shape[1], probe.shape[1] // 2), F32)],
        compiler_params=pltpu.CompilerParams(vmem_limit_bytes=44 * 1024 * 1024),
        name="misfit",
    )(positions, counts, field, probe, patterns, table)


def radices(count):
    out = []
    while count > 1:
        out.append(4 if len(out) >= 2 and count % 4 == 0 else 2)
        count //= out[-1]
    return out


def signal(peer):
    pl.semaphore_signal(
        pltpu.get_barrier_semaphore(), inc=1, device_id={"row": peer}, device_id_type=pl.DeviceIdType.MESH
    )


def remote(source, target, send, recv, peer):
    return pltpu.make_async_remote_copy(
        src_ref=source,
        dst_ref=target,
        send_sem=send,
        recv_sem=recv,
        device_id={"row": peer},
        device_id_type=pl.DeviceIdType.MESH,
    )


def both_sides(me, count, action):
    @pl.when(me > 0)
    def _():
        action(0)

    @pl.when(me < count - 1)
    def _():
        action(1)


def neighbours(me, count):
    return lax.min(me, 1) + lax.min(count - 1 - me, 1)


def border_kernel(count, own, field, send, recv, here):
    me = lax.axis_index("row")
    tile = own.shape[1]
    h = (field.shape[1] - tile) // 2
    up, down = lax.max(me - 1, 0), lax.min(me + 1, count - 1)
    low, high = field.at[:, :h], field.at[:, h + tile :]
    move = pltpu.make_async_copy(own, field.at[:, h : h + tile], here)
    copies = (
        remote(own.at[:, :h], high, send.at[0], recv.at[1], up),
        remote(own.at[:, tile - h :], low, send.at[1], recv.at[0], down),
    )
    arrivals = (
        remote(own.at[:, :h], low, send.at[0], recv.at[0], up),
        remote(own.at[:, :h], high, send.at[1], recv.at[1], down),
    )
    both_sides(me, count, lambda side: signal((up, down)[side]))
    pl.semaphore_wait(pltpu.get_barrier_semaphore(), neighbours(me, count))
    both_sides(me, count, lambda side: copies[side].start())
    move.start()

    @pl.when(me == 0)
    def _():
        field[:, :h] = jnp.zeros((2, h, field.shape[2]), F32)

    @pl.when(me == count - 1)
    def _():
        field[:, h + tile :] = jnp.zeros((2, h, field.shape[2]), F32)

    move.wait()
    both_sides(me, count, lambda side: arrivals[side].wait_recv())
    both_sides(me, count, lambda side: copies[side].wait_send())


def border_call(own, h, count):
    field = jax.ShapeDtypeStruct((own.shape[0], own.shape[1] + 2 * h, own.shape[2]), F32)
    return pl.pallas_call(
        functools.partial(border_kernel, count),
        out_shape=field,
        in_specs=[pl.BlockSpec(memory_space=pl.ANY)],
        out_specs=pl.BlockSpec(memory_space=pltpu.VMEM),
        scratch_shapes=[pltpu.SemaphoreType.DMA((2,)), pltpu.SemaphoreType.DMA((2,)), pltpu.SemaphoreType.DMA],
        compiler_params=pltpu.CompilerParams(
            collective_id=0, has_side_effects=True, vmem_limit_bytes=16 * 1024 * 1024
        ),
        cost_estimate=pl.CostEstimate(flops=10**10, bytes_accessed=8 * 1024 * 1024, transcendentals=0),
        name="border",
    )(own)


def sums_kernel(count, grads, probe, out, out_probe, from_above, from_below, *scratch):
    me = lax.axis_index("row")
    tile = out.shape[1]
    h = from_above.shape[1]
    grad_low, grad_high = grads.at[:, :h], grads.at[:, h + tile :]
    steps = radices(count)
    halo_send, halo_recv, rs_send, rs_recv, ag_send, ag_recv = scratch[:6]
    held = scratch[6 : 6 + len(steps)]
    landed = scratch[6 + len(steps) :]
    up, down = lax.max(me - 1, 0), lax.min(me + 1, count - 1)

    levels = []
    stride, size, start = 1, probe.shape[0], 0
    index = 0
    for radix in steps:
        digit = lax.rem(me // stride, radix)
        size //= radix
        others = []
        for k in range(1, radix):
            other = lax.rem(digit + k, radix)
            others.append((index, k, other, me + (other - digit) * stride))
            index += 1
        levels.append((radix, digit, size, start, others))
        start = start + digit * size
        stride *= radix

    both_sides(me, count, lambda side: signal((up, down)[side]))
    for level in levels:
        for _, _, _, peer in level[4]:
            signal(peer)
    pl.semaphore_wait(pltpu.get_barrier_semaphore(), index + neighbours(me, count))

    halos = (
        remote(grad_low, from_below, halo_send.at[0], halo_recv.at[1], up),
        remote(grad_high, from_above, halo_send.at[1], halo_recv.at[0], down),
    )
    arrivals = (
        remote(grad_low, from_above, halo_send.at[0], halo_recv.at[0], up),
        remote(grad_high, from_below, halo_send.at[1], halo_recv.at[1], down),
    )

    def rs_copies(depth):
        radix, digit, size, _, others = levels[depth]
        source = probe if depth == 0 else held[depth - 1]
        return [
            remote(
                source.at[pl.ds(pl.multiple_of(other * size, 8), size)],
                landed[depth].at[radix - 1 - k],
                rs_send.at[i],
                rs_recv.at[levels[depth][4][radix - 1 - k][0]],
                peer,
            )
            for i, k, other, peer in others
        ]

    def rs_arrivals(depth):
        radix, digit, size, _, others = levels[depth]
        source = probe if depth == 0 else held[depth - 1]
        return [
            remote(source.at[pl.ds(0, size)], landed[depth].at[k - 1], rs_send.at[i], rs_recv.at[i], peer)
            for i, k, other, peer in others
        ]

    started = []
    for depth, (radix, digit, size, _, others) in enumerate(levels):
        copies = rs_copies(depth)
        for copy in copies:
            copy.start()
        started += copies
        if depth == min(1, len(levels) - 1):
            both_sides(me, count, lambda side: halos[side].start())
            out[...] = grads[:, h : h + tile]
        source = probe if depth == 0 else held[depth - 1]
        value = source[pl.ds(pl.multiple_of(digit * size, 8), size)]
        for k, arrival in enumerate(rs_arrivals(depth)):
            arrival.wait_recv()
            value = value + landed[depth][k]
        held[depth][...] = value

    mine = pl.ds(pl.multiple_of(start, 8), levels[-1][2])
    out_probe[mine] = held[-1][...]
    for depth in reversed(range(len(levels))):
        radix, digit, size, first, others = levels[depth]
        region = pl.ds(pl.multiple_of(first + digit * size, 8), size)
        copies = [
            remote(
                out_probe.at[region],
                out_probe.at[region],
                ag_send.at[i],
                ag_recv.at[others[radix - 1 - k][0]],
                peer,
            )
            for i, k, other, peer in others
        ]
        for copy in copies:
            copy.start()
        started += copies
        for i, k, other, peer in others:
            theirs = pl.ds(pl.multiple_of(first + other * size, 8), size)
            remote(out_probe.at[region], out_probe.at[theirs], ag_send.at[i], ag_recv.at[i], peer).wait_recv()

    def add_side(side):
        arrivals[side].wait_recv()
        where, value = ((slice(0, h), from_above), (slice(tile - h, tile), from_below))[side]
        out[:, where] += value[...]

    both_sides(me, count, add_side)
    for copy in started:
        copy.wait_send()
    both_sides(me, count, lambda side: halos[side].wait_send())


def sums_call(grads, probe, h, count):
    vmem = pl.BlockSpec(memory_space=pltpu.VMEM)
    steps = radices(count)
    pieces = sum(radix - 1 for radix in steps)
    held, landed, size = [], [], probe.shape[0]
    for radix in steps:
        size //= radix
        held.append(pltpu.VMEM((size, probe.shape[1]), F32))
        landed.append(pltpu.VMEM((radix - 1, size, probe.shape[1]), F32))
    return pl.pallas_call(
        functools.partial(sums_kernel, count),
        out_shape=(jax.ShapeDtypeStruct((grads.shape[0], grads.shape[1] - 2 * h, grads.shape[2]), F32), jax.ShapeDtypeStruct(probe.shape, F32)),
        in_specs=[vmem] * 2,
        out_specs=(vmem, vmem),
        scratch_shapes=[pltpu.VMEM((grads.shape[0], h, grads.shape[2]), F32)] * 2
        + [pltpu.SemaphoreType.DMA((2,))] * 2
        + [pltpu.SemaphoreType.DMA((pieces,))] * 4
        + held
        + landed,
        compiler_params=pltpu.CompilerParams(
            collective_id=1, has_side_effects=True, vmem_limit_bytes=40 * 1024 * 1024
        ),
        name="sums",
    )(grads, probe)


def local(object_field, probe_wave, patterns, positions, counts):
    extent = probe_wave.shape[1]
    h = extent // 2
    size = lax.axis_size("row")
    table = jnp.asarray(tables(extent))
    field = border_call(object_field, h, size)
    grads, grad_probe = misfit_call(positions, counts, field, probe_wave, patterns, table)
    grads, grad_probe = sums_call(grads, grad_probe.reshape(-1, extent), h, size)
    return grads, grad_probe.reshape(probe_wave.shape)


def solution(mesh):
    placed = (
        P(None, ("groups", "row"), None),
        P(None, "groups", None),
        P(("groups", "row"), None, None),
        P(("groups", "row"), None),
        P("groups"),
    )
    return jax.shard_map(
        local,
        mesh=mesh,
        in_specs=placed,
        out_specs=(P(None, ("groups", "row"), None), P(None, "groups", None)),
        check_vma=False,
    )
```

```python
import functools
import math

import jax
import jax.numpy as jnp
import ml_dtypes
import numpy as np
from jax import lax
from jax.experimental import pallas as pl
from jax.experimental.pallas import tpu as pltpu
from jax.sharding import PartitionSpec as P

F32 = jnp.float32
BF16 = jnp.bfloat16
WIDTH = 4
PIECES = 4


def tables(extent):
    half = extent // 2
    line = np.arange(half)
    out = []
    for parity in (0, 1):
        angle = ((2 * line[:, None] + parity) * line[None, :] % extent) * (2.0 * math.pi / extent)
        cos, sin = np.cos(angle) / math.sqrt(extent), np.sin(angle) / math.sqrt(extent)
        full = np.block([[cos, sin], [-sin, cos]])
        for matrix in (full, full.T):
            high = matrix.astype(ml_dtypes.bfloat16)
            low = (matrix - high.astype(np.float64)).astype(ml_dtypes.bfloat16)
            out += [high, low]
    order = np.zeros((extent, extent), np.float32)
    order[2 * line, line] = 1
    order[2 * line + 1, half + line] = 1
    out.append(order.astype(ml_dtypes.bfloat16))
    return np.stack(out)


def parts(value):
    high = value.astype(BF16)
    return high, (value - high.astype(F32)).astype(BF16)


def dot(left, right):
    return jnp.dot(left, right, preferred_element_type=F32)


def from_left(table, index, value):
    high, low = parts(value)
    return dot(
        jnp.concatenate([table[index], table[index], table[index + 1]], axis=1),
        jnp.concatenate([high, low, high], axis=0),
    )


def from_right(value, table, index):
    high, low = parts(value)
    return dot(
        jnp.concatenate([high, low, high], axis=1),
        jnp.concatenate([table[index], table[index], table[index + 1]], axis=0),
    )


def lanes(*blocks):
    return jnp.concatenate(blocks, axis=1)


def rows(*blocks):
    return jnp.concatenate(blocks, axis=0)


def transform(re, im, table):
    h = re.shape[0] // 2
    even = from_right(lanes(re[:, :h] + re[:, h:], im[:, :h] + im[:, h:]), table, 2)
    odd = from_right(lanes(re[:, :h] - re[:, h:], im[:, :h] - im[:, h:]), table, 6)
    re, im = lanes(even[:, :h], odd[:, :h]), lanes(even[:, h:], odd[:, h:])
    even = from_left(table, 0, rows(re[:h] + re[h:], im[:h] + im[h:]))
    odd = from_left(table, 4, rows(re[:h] - re[h:], im[:h] - im[h:]))
    return even, odd


def inverse(even, odd, table):
    h = even.shape[0] // 2
    total = from_left(table, 2, even)
    other = from_left(table, 6, odd)
    top, low = total + other, total - other
    even = from_right(rows(lanes(top[:h, :h], top[h:, :h]), lanes(low[:h, :h], low[h:, :h])), table, 0)
    odd = from_right(rows(lanes(top[:h, h:], top[h:, h:]), lanes(low[:h, h:], low[h:, h:])), table, 4)
    total, other = even + odd, even - odd
    return lanes(total[:, :h], other[:, :h]), lanes(total[:, h:], other[:, h:])


def turned_rows(value, amount, up):
    groups = value.reshape(value.shape[0] // 8, 8, value.shape[1])
    place = lax.broadcasted_iota(jnp.int32, groups.shape, 1)
    if up:
        inner = pltpu.roll(groups, lax.rem(8 - amount, 8), 1)
        other = jnp.concatenate([inner[1:], inner[:1]], axis=0)
        result = jnp.where(place < 8 - amount, inner, other)
    else:
        inner = pltpu.roll(groups, amount, 1)
        other = jnp.concatenate([inner[-1:], inner[:-1]], axis=0)
        result = jnp.where(place >= amount, inner, other)
    return result.reshape(value.shape)


def misfit_kernel(positions, counts, field, probe, patterns, table, total, grad_probe, ordered):
    extent = probe.shape[1]
    h = extent // 2
    tile = field.shape[1] - extent
    me = lax.axis_index("row")
    live = counts[me]
    total[...] = jnp.zeros_like(total)
    grad_probe[...] = jnp.zeros_like(grad_probe)
    column = lax.broadcasted_iota(jnp.int32, (extent, extent), 1)

    def load(slot):
        first = positions[slot, 0] - (me * tile - h)
        shift = positions[slot, 1]
        kept = column >= shift
        sub = lax.rem(first, 8)
        base = pl.multiple_of(first - sub, 8)
        at = pl.ds(base, extent)
        after = pl.ds(pl.multiple_of(base + extent, 8), 8)
        inside = lax.broadcasted_iota(jnp.int32, (8, extent), 0) >= sub

        def patch_of(i):
            body = jnp.where(kept, field[i, at, :extent], field[i, at, extent:])
            wrap = jnp.where(kept[:8], field[i, after, :extent], field[i, after, extent:])
            return rows(jnp.where(inside, body[:8], wrap), body[8:])

        patch = [patch_of(i) for i in (0, 1)]
        turned = [
            turned_rows(pltpu.roll(probe[i], lax.rem(shift, extent), 1), sub, False) for i in (0, 1)
        ]
        return shift, kept, sub, at, after, inside, patch, turned

    def gradient(slot, lane, patch, turned):
        even, odd = transform(
            turned[0] * patch[0] - turned[1] * patch[1], turned[0] * patch[1] + turned[1] * patch[0], table
        )
        permuted = dot(lanes(*parts(patterns[slot])), rows(table[8], table[8]))
        ordered[lane, 0] = permuted[:, :h]
        ordered[lane, 1] = permuted[:, h:]
        alive = (slot < live).astype(F32)
        results = []
        for parity, value in ((0, even), (1, odd)):
            picked = pl.ds(parity, h, 2)
            pattern = lanes(ordered[lane, 0, picked, :], ordered[lane, 1, picked, :])
            gap = (value[:h] * value[:h] + value[h:] * value[h:] - pattern) * alive
            results.append(rows(gap * value[:h], gap * value[h:]))
        return inverse(results[0], results[1], table)

    def add(where, patch, turned, re, im):
        shift, kept, sub, at, after, inside = where
        zero = jnp.zeros_like(re)
        grads = (turned[0] * re + turned[1] * im, turned[0] * im - turned[1] * re)
        for i in (0, 1):
            body = rows(jnp.where(inside, grads[i][:8], zero[:8]), grads[i][8:])
            wrap = jnp.where(inside, zero[:8], grads[i][:8])
            total[i, at, :extent] += jnp.where(kept, body, zero)
            total[i, at, extent:] += jnp.where(kept, zero, body)
            total[i, after, :extent] += jnp.where(kept[:8], wrap, zero[:8])
            total[i, after, extent:] += jnp.where(kept[:8], zero[:8], wrap)
        back = lax.rem(extent - lax.rem(shift, extent), extent)
        for i, value in enumerate((patch[0] * re + patch[1] * im, patch[0] * im - patch[1] * re)):
            grad_probe[i] += turned_rows(pltpu.roll(value, back, 1), sub, True)

    def step(group, carry):
        slots = [group * WIDTH + lane for lane in range(WIDTH)]
        loaded = [load(slot) for slot in slots]
        grads = [gradient(slot, lane, *loaded[lane][6:]) for lane, slot in enumerate(slots)]
        for one, (re, im) in zip(loaded, grads):
            add(one[:6], one[6], one[7], re, im)
        return carry

    lax.fori_loop(0, (live + WIDTH - 1) // WIDTH, step, 0)


def misfit_call(positions, counts, field, probe, patterns, table):
    vmem = pl.BlockSpec(memory_space=pltpu.VMEM)
    smem = pl.BlockSpec(memory_space=pltpu.SMEM)
    return pl.pallas_call(
        misfit_kernel,
        out_shape=(jax.ShapeDtypeStruct(field.shape, F32), jax.ShapeDtypeStruct(probe.shape, F32)),
        in_specs=[smem, smem] + [vmem] * 4,
        out_specs=(vmem, vmem),
        scratch_shapes=[pltpu.VMEM((WIDTH, 2, probe.shape[1], probe.shape[1] // 2), F32)],
        compiler_params=pltpu.CompilerParams(vmem_limit_bytes=44 * 1024 * 1024),
        name="misfit",
    )(positions, counts, field, probe, patterns, table)


def radices(count):
    out = []
    while count > 1:
        out.append(4 if len(out) >= 2 and count % 4 == 0 else 2)
        count //= out[-1]
    return out


def signal(peer):
    pl.semaphore_signal(
        pltpu.get_barrier_semaphore(), inc=1, device_id={"row": peer}, device_id_type=pl.DeviceIdType.MESH
    )


def remote(source, target, send, recv, peer):
    return pltpu.make_async_remote_copy(
        src_ref=source,
        dst_ref=target,
        send_sem=send,
        recv_sem=recv,
        device_id={"row": peer},
        device_id_type=pl.DeviceIdType.MESH,
    )


def both_sides(me, count, action):
    @pl.when(me > 0)
    def _():
        action(0)

    @pl.when(me < count - 1)
    def _():
        action(1)


def neighbours(me, count):
    return lax.min(me, 1) + lax.min(count - 1 - me, 1)


def border_kernel(count, own, field, send, recv, here):
    me = lax.axis_index("row")
    tile = own.shape[1]
    h = (field.shape[1] - tile) // 2
    up, down = lax.max(me - 1, 0), lax.min(me + 1, count - 1)
    low, high = field.at[:, :h], field.at[:, h + tile :]
    move = pltpu.make_async_copy(own, field.at[:, h : h + tile], here)
    copies = (
        remote(own.at[:, :h], high, send.at[0], recv.at[1], up),
        remote(own.at[:, tile - h :], low, send.at[1], recv.at[0], down),
    )
    arrivals = (
        remote(own.at[:, :h], low, send.at[0], recv.at[0], up),
        remote(own.at[:, :h], high, send.at[1], recv.at[1], down),
    )
    both_sides(me, count, lambda side: signal((up, down)[side]))
    pl.semaphore_wait(pltpu.get_barrier_semaphore(), neighbours(me, count))
    both_sides(me, count, lambda side: copies[side].start())
    move.start()

    @pl.when(me == 0)
    def _():
        field[:, :h] = jnp.zeros((2, h, field.shape[2]), F32)

    @pl.when(me == count - 1)
    def _():
        field[:, h + tile :] = jnp.zeros((2, h, field.shape[2]), F32)

    move.wait()
    both_sides(me, count, lambda side: arrivals[side].wait_recv())
    both_sides(me, count, lambda side: copies[side].wait_send())


def border_call(own, h, count):
    field = jax.ShapeDtypeStruct((own.shape[0], own.shape[1] + 2 * h, own.shape[2]), F32)
    return pl.pallas_call(
        functools.partial(border_kernel, count),
        out_shape=field,
        in_specs=[pl.BlockSpec(memory_space=pl.ANY)],
        out_specs=pl.BlockSpec(memory_space=pltpu.VMEM),
        scratch_shapes=[pltpu.SemaphoreType.DMA((2,)), pltpu.SemaphoreType.DMA((2,)), pltpu.SemaphoreType.DMA],
        compiler_params=pltpu.CompilerParams(
            collective_id=0, has_side_effects=True, vmem_limit_bytes=16 * 1024 * 1024
        ),
        cost_estimate=pl.CostEstimate(flops=10**10, bytes_accessed=8 * 1024 * 1024, transcendentals=0),
        name="border",
    )(own)


def sums_kernel(count, grads, probe, out, out_probe, from_above, from_below, *scratch):
    me = lax.axis_index("row")
    tile = out.shape[1]
    h = from_above.shape[1]
    grad_low, grad_high = grads.at[:, :h], grads.at[:, h + tile :]
    steps = radices(count)
    halo_send, halo_recv, rs_send, rs_recv, ag_send, ag_recv = scratch[:6]
    held = scratch[6 : 6 + len(steps)]
    landed = scratch[6 + len(steps) :]
    up, down = lax.max(me - 1, 0), lax.min(me + 1, count - 1)

    levels = []
    stride, size, start = 1, probe.shape[0], 0
    index = 0
    for radix in steps:
        digit = lax.rem(me // stride, radix)
        size //= radix
        others = []
        for k in range(1, radix):
            other = lax.rem(digit + k, radix)
            others.append((index, k, other, me + (other - digit) * stride))
            index += 1
        levels.append((radix, digit, size, start, others))
        start = start + digit * size
        stride *= radix

    both_sides(me, count, lambda side: signal((up, down)[side]))
    for level in levels:
        for _, _, _, peer in level[4]:
            signal(peer)
    pl.semaphore_wait(pltpu.get_barrier_semaphore(), index + neighbours(me, count))

    part = h // PIECES

    def piece(ref, k):
        return ref.at[:, k * part : (k + 1) * part]

    halos, arrivals = [], []
    for k in range(PIECES):
        low, high = piece(grad_low, k), piece(grad_high, k)
        above, below = piece(from_above, k), piece(from_below, k)
        halos.append(
            (
                remote(low, below, halo_send.at[0, k], halo_recv.at[1, k], up),
                remote(high, above, halo_send.at[1, k], halo_recv.at[0, k], down),
            )
        )
        arrivals.append(
            (
                remote(low, above, halo_send.at[0, k], halo_recv.at[0, k], up),
                remote(high, below, halo_send.at[1, k], halo_recv.at[1, k], down),
            )
        )

    def send_halo(k):
        both_sides(me, count, lambda side: halos[k][side].start())

    def rs_copies(depth):
        radix, digit, size, _, others = levels[depth]
        source = probe if depth == 0 else held[depth - 1]
        return [
            remote(
                source.at[pl.ds(pl.multiple_of(other * size, 8), size)],
                landed[depth].at[radix - 1 - k],
                rs_send.at[i],
                rs_recv.at[levels[depth][4][radix - 1 - k][0]],
                peer,
            )
            for i, k, other, peer in others
        ]

    def rs_arrivals(depth):
        radix, digit, size, _, others = levels[depth]
        source = probe if depth == 0 else held[depth - 1]
        return [
            remote(source.at[pl.ds(0, size)], landed[depth].at[k - 1], rs_send.at[i], rs_recv.at[i], peer)
            for i, k, other, peer in others
        ]

    started = []
    sent = 0
    for depth, (radix, digit, size, _, others) in enumerate(levels):
        copies = rs_copies(depth)
        for copy in copies:
            copy.start()
        started += copies
        if depth >= 1 and sent < PIECES:
            send_halo(sent)
            sent += 1
        if depth == 0:
            out[...] = grads[:, h : h + tile]
        source = probe if depth == 0 else held[depth - 1]
        value = source[pl.ds(pl.multiple_of(digit * size, 8), size)]
        for k, arrival in enumerate(rs_arrivals(depth)):
            arrival.wait_recv()
            value = value + landed[depth][k]
        held[depth][...] = value

    mine = pl.ds(pl.multiple_of(start, 8), levels[-1][2])
    out_probe[mine] = held[-1][...]
    for depth in reversed(range(len(levels))):
        radix, digit, size, first, others = levels[depth]
        region = pl.ds(pl.multiple_of(first + digit * size, 8), size)
        copies = [
            remote(
                out_probe.at[region],
                out_probe.at[region],
                ag_send.at[i],
                ag_recv.at[others[radix - 1 - k][0]],
                peer,
            )
            for i, k, other, peer in others
        ]
        for copy in copies:
            copy.start()
        started += copies
        while sent < PIECES:
            send_halo(sent)
            sent += 1
            if depth > 1:
                break
        for i, k, other, peer in others:
            theirs = pl.ds(pl.multiple_of(first + other * size, 8), size)
            remote(out_probe.at[region], out_probe.at[theirs], ag_send.at[i], ag_recv.at[i], peer).wait_recv()

    def add_side(side):
        for k in range(PIECES):
            arrivals[k][side].wait_recv()
        where, value = ((slice(0, h), from_above), (slice(tile - h, tile), from_below))[side]
        out[:, where] += value[...]

    both_sides(me, count, add_side)
    for copy in started:
        copy.wait_send()
    for k in range(PIECES):
        both_sides(me, count, lambda side: halos[k][side].wait_send())


def sums_call(grads, probe, h, count):
    vmem = pl.BlockSpec(memory_space=pltpu.VMEM)
    steps = radices(count)
    pieces = sum(radix - 1 for radix in steps)
    held, landed, size = [], [], probe.shape[0]
    for radix in steps:
        size //= radix
        held.append(pltpu.VMEM((size, probe.shape[1]), F32))
        landed.append(pltpu.VMEM((radix - 1, size, probe.shape[1]), F32))
    return pl.pallas_call(
        functools.partial(sums_kernel, count),
        out_shape=(jax.ShapeDtypeStruct((grads.shape[0], grads.shape[1] - 2 * h, grads.shape[2]), F32), jax.ShapeDtypeStruct(probe.shape, F32)),
        in_specs=[vmem] * 2,
        out_specs=(vmem, vmem),
        scratch_shapes=[pltpu.VMEM((grads.shape[0], h, grads.shape[2]), F32)] * 2
        + [pltpu.SemaphoreType.DMA((2, PIECES))] * 2
        + [pltpu.SemaphoreType.DMA((pieces,))] * 4
        + held
        + landed,
        compiler_params=pltpu.CompilerParams(
            collective_id=1, has_side_effects=True, vmem_limit_bytes=40 * 1024 * 1024
        ),
        name="sums",
    )(grads, probe)


def local(object_field, probe_wave, patterns, positions, counts):
    extent = probe_wave.shape[1]
    h = extent // 2
    size = lax.axis_size("row")
    table = jnp.asarray(tables(extent))
    field = border_call(object_field, h, size)
    grads, grad_probe = misfit_call(positions, counts, field, probe_wave, patterns, table)
    grads, grad_probe = sums_call(grads, grad_probe.reshape(-1, extent), h, size)
    return grads, grad_probe.reshape(probe_wave.shape)


def solution(mesh):
    placed = (
        P(None, ("groups", "row"), None),
        P(None, "groups", None),
        P(("groups", "row"), None, None),
        P(("groups", "row"), None),
        P("groups"),
    )
    return jax.shard_map(
        local,
        mesh=mesh,
        in_specs=placed,
        out_specs=(P(None, ("groups", "row"), None), P(None, "groups", None)),
        check_vma=False,
    )
```
